32 devices in a mesh: dp: 1, mp: 32 (over z, y, x, core).
Axes of the slice: x: 2, y: 2, z: 4, core: 2. Of those that a mesh axis runs over, the one named last changes fastest.
Arguments:
- grads: bfloat16 [1, 16, 32, 256, 256], P('dp', None, 'mp'), may hold values from -18 to 18
- layer_map: int32 [512], replicated, may hold values from 0 to 31, never falling along the last dimension, each value on 1 to 32 neighbouring positions
Outputs:
- roots: float32 [16, 32, 256, 256], P(None, 'mp', 'dp')
The draws below stay inside these ranges and needn't reach their ends.
Inputs may be any that keep to these rules, and one draw needn't show every extreme that they name: `layer_map`: layer numbers never fall along b; every layer 0 to 31 holds 1 to 32 blocks.
All inputs are finite; a program needn't handle non-finite values.
Results may differ from the reference program's by a relative error of at most 0.0003.
Values sent between devices are 32-bit elements; how exact they have to be, the bound alone decides.
A program may use at most 64 MiB of HBM per device.

```python
import math
import jax
import jax.numpy as jnp
import numpy as np
from jax import lax

ORDER = 256
COLS = 256
BLOCKS_HELD = 16
ITERS = 8
REPLICAS = 1
HOLDERS = 32
LAYERS = 32
BLOCKS = 512


def draw_grads(key, part):
    shape = (REPLICAS, BLOCKS_HELD, HOLDERS, ORDER, COLS)
    first, second = jax.random.split(jax.random.fold_in(key, 17), 2)
    base = jnp.clip(jax.random.normal(first, shape, jnp.float32), -6.0, 6.0)
    logscale = jax.random.uniform(second, (1, BLOCKS_HELD, HOLDERS, ORDER, 1), jnp.float32, math.log(0.3), math.log(3.0))
    return (base * jnp.exp(logscale)).astype(jnp.bfloat16)


def length_profile(amount, total, reach, slope):
    loads = [(1 << 20) // math.isqrt(standing ** slope) + 1 for standing in range(2, amount + 1)]
    surplus, given = total - reach - (amount - 1), [1] * (amount - 1)
    while surplus > 0:
        free = [i for i in range(amount - 1) if given[i] < reach]
        whole, budget = sum([loads[i] for i in free]), surplus
        for i in free:
            more = min(reach - given[i], max(1, budget * loads[i] // whole), surplus)
            given[i] = given[i] + more
            surplus = surplus - more
    return np.array([reach] + given)


def ragged(stream_key, number_of, total, limit, skew):
    if number_of == 2:
        one = jax.random.randint(stream_key, (), max(1, total - limit), min(limit, total - 1) + 1)
        return jnp.stack([one, total - one])
    lengths = jnp.asarray(length_profile(number_of, total, limit, skew), jnp.int32)
    pairs = (number_of - 1) // 2
    donor, sink = lengths[1:1 + 2 * pairs:2], lengths[2:2 + 2 * pairs:2]
    margin = jnp.minimum(donor - 1, limit - sink)
    passed = jax.random.randint(jax.random.fold_in(stream_key, 1), (pairs,), 0, 1 << 20) % (margin + 1)
    lengths = lengths.at[1:1 + 2 * pairs:2].set(donor - passed).at[2:2 + 2 * pairs:2].set(sink + passed)
    return lengths[jax.random.permutation(jax.random.fold_in(stream_key, 2), number_of)]


def setup_inputs(seed: int = 0) -> dict:
    splits = jax.random.split(jax.random.key(seed), 3)
    return {
        "grads": draw_grads(jax.random.fold_in(splits[2], 71), 0),
        "layer_map": jnp.searchsorted(jnp.cumsum(ragged(splits[1], LAYERS, BLOCKS, LAYERS, 2)), jnp.arange(BLOCKS), side="right").astype(jnp.int32),
    }


def newton_root(stats, ridge, live):
    order = stats.shape[-1]
    identity = jnp.eye(order, dtype=jnp.float32)
    damped = jnp.where(live[:, None, None], stats + ridge[:, None, None] * identity, identity)
    frobenius = jnp.sqrt(lax.optimization_barrier(jnp.sum(damped * damped, axis=(1, 2))))
    scaled = 2.5 / frobenius
    current = (scaled ** 0.25)[:, None, None] * identity
    coupled = scaled[:, None, None] * damped
    for _ in range(ITERS):
        factor = 1.25 * identity - 0.25 * coupled
        current = jnp.einsum('sij,sjk->sik', current, factor, precision=lax.Precision.HIGHEST)
        square = jnp.einsum('sij,sjk->sik', factor, factor, precision=lax.Precision.HIGHEST)
        fourth = jnp.einsum('sij,sjk->sik', square, square, precision=lax.Precision.HIGHEST)
        coupled = jnp.einsum('sij,sjk->sik', fourth, coupled, precision=lax.Precision.HIGHEST)
    return current

def reference(grads, layer_map):
    replicas = grads.shape[0]
    order = grads.shape[3]
    columns = grads.shape[4]
    flat = grads.reshape(replicas, BLOCKS, order, columns)

    def stat_block(pieces):
        wide = pieces.astype(jnp.float32)
        return jnp.einsum('ric,rjc->ij', wide, wide, precision=lax.Precision.HIGHEST) / (replicas * columns)
    stats = lax.map(stat_block, jnp.moveaxis(flat, 1, 0))
    traces = jnp.trace(stats, axis1=1, axis2=2)
    layer_ids = jnp.arange(LAYERS, dtype=jnp.int32)
    onehot = (layer_map[:, None] == layer_ids[None, :]).astype(jnp.float32)
    totals = jnp.dot(traces, onehot, precision=lax.Precision.HIGHEST)
    counts = lax.optimization_barrier(jnp.sum(onehot, axis=0))
    layer_ridge = 0.1 * totals / (counts * order)
    block_ridge = jnp.dot(onehot, layer_ridge, precision=lax.Precision.HIGHEST)
    live = jnp.ones((BLOCKS,), dtype=bool)
    roots = newton_root(stats, block_ridge, live)
    return roots.reshape(BLOCKS_HELD, HOLDERS, order, order)
```

```python
import functools

import jax
import jax.numpy as jnp
from jax import lax
from jax.experimental import pallas as pl
from jax.experimental.pallas import tpu as pltpu
from jax.sharding import PartitionSpec as P

ITERS = 8


def newton_root(stats, ridge, live):
    order = stats.shape[-1]
    identity = jnp.eye(order, dtype=jnp.float32)
    damped = jnp.where(live[:, None, None], stats + ridge[:, None, None] * identity, identity)
    frobenius = jnp.sqrt(jnp.sum(damped * damped, axis=(1, 2)))
    scaled = 2.5 / frobenius
    current = (scaled**0.25)[:, None, None] * identity
    coupled = scaled[:, None, None] * damped
    for _ in range(ITERS):
        factor = 1.25 * identity - 0.25 * coupled
        current = jnp.einsum("sij,sjk->sik", current, factor, precision=lax.Precision.HIGHEST)
        square = jnp.einsum("sij,sjk->sik", factor, factor, precision=lax.Precision.HIGHEST)
        fourth = jnp.einsum("sij,sjk->sik", square, square, precision=lax.Precision.HIGHEST)
        coupled = jnp.einsum("sij,sjk->sik", fourth, coupled, precision=lax.Precision.HIGHEST)
    return current


def local_split(grads, layer_map):
    gradient = grads[0, :, 0]
    blocks_here, order, columns = gradient.shape
    replicas = lax.axis_size("dp")
    holders = lax.axis_size("mp")
    band = order // replicas
    replica = lax.axis_index("dp")
    holder = lax.axis_index("mp")
    partial_value = jnp.einsum(
        "bic,bjc->bij", gradient, gradient, preferred_element_type=jnp.float32
    ) * (1.0 / (replicas * columns))
    summed = lax.psum(partial_value, "dp")
    mine = lax.dynamic_slice_in_dim(summed, replica * band, band, 1)
    layer_grid = layer_map.reshape(blocks_here, holders)
    my_layers = lax.dynamic_slice_in_dim(layer_grid, holder, 1, 1)[:, 0]
    layer_ids = jnp.arange(holders, dtype=jnp.int32)
    local_onehot = (my_layers[:, None] == layer_ids[None, :]).astype(jnp.float32)
    all_counts = jnp.sum((layer_map[:, None] == layer_ids[None, :]).astype(jnp.int32), axis=0)
    diag_rows = lax.dynamic_slice_in_dim(mine, replica * band, band, 2)
    diag_part = jnp.trace(diag_rows, axis1=1, axis2=2)
    layer_part = jnp.dot(diag_part, local_onehot, precision=lax.Precision.HIGHEST)
    layer_total = lax.psum(layer_part, ("dp", "mp"))
    layer_ridge = 0.1 * layer_total / (all_counts.astype(jnp.float32) * order)
    spread = -(-blocks_here // replicas)
    extra = replicas * spread - blocks_here
    stacked = lax.all_to_all(mine, "dp", split_axis=0, concat_axis=1, tiled=True)
    block_ridge = jnp.pad(
        jnp.dot(local_onehot, layer_ridge, precision=lax.Precision.HIGHEST), (0, extra)
    )
    slot_ridge = lax.dynamic_slice_in_dim(block_ridge, replica * spread, spread, 0)
    slot_index = replica * spread + jnp.arange(spread, dtype=jnp.int32)
    solved = newton_root(stacked, slot_ridge, slot_index < blocks_here)
    returned = lax.all_to_all(solved, "dp", split_axis=1, concat_axis=0, tiled=True)
    result = returned[:blocks_here]
    return result.reshape(blocks_here, 1, band, order)


LANES = 128
TOGETHER = 2
RECENTRE = (2, 4, 6)


def trace_exchange(holders, grad_ref, total_ref, slots, send_sem, recv_sem):
    me = lax.axis_index("mp")
    peers = [lax.rem(me + step, holders) for step in range(1, holders)]
    barrier = pltpu.get_barrier_semaphore()
    for peer in peers:
        pl.semaphore_signal(
            barrier, inc=1, device_id={"mp": peer}, device_id_type=pl.DeviceIdType.MESH
        )
    blocks_here, _, columns = grad_ref.shape
    shape = total_ref.shape
    place = lax.broadcasted_iota(jnp.int32, shape, 0) * LANES + lax.broadcasted_iota(
        jnp.int32, shape, 1
    )
    mine = jnp.zeros(shape, jnp.float32)
    for i in range(blocks_here):
        wide = grad_ref[i].astype(jnp.float32)
        rows = jnp.sum(wide * wide, axis=0, keepdims=True)
        trace = jnp.sum(rows, axis=1, keepdims=True) * (1.0 / columns)
        mine = jnp.where(place == i * holders + me, trace, mine)
    slots[me] = mine
    pl.semaphore_wait(barrier, holders - 1)
    copies = []
    for peer in peers:
        copy = pltpu.make_async_remote_copy(
            src_ref=slots.at[me],
            dst_ref=slots.at[me],
            send_sem=send_sem.at[peer],
            recv_sem=recv_sem.at[me],
            device_id={"mp": peer},
            device_id_type=pl.DeviceIdType.MESH,
        )
        copy.start()
        copies.append(copy)
    for peer in peers:
        pltpu.make_async_remote_copy(
            src_ref=slots.at[peer],
            dst_ref=slots.at[peer],
            send_sem=send_sem.at[peer],
            recv_sem=recv_sem.at[peer],
            device_id={"mp": peer},
            device_id_type=pl.DeviceIdType.MESH,
        ).wait_recv()
    total = slots[0]
    for i in range(1, holders):
        total = total + slots[i]
    total_ref[...] = total
    for copy in copies:
        copy.wait_send()


def exchange_traces(gradient, holders, blocks):
    rows = -(-blocks // (8 * LANES)) * 8
    return pl.pallas_call(
        functools.partial(trace_exchange, holders),
        out_shape=jax.ShapeDtypeStruct((rows, LANES), jnp.float32),
        in_specs=[pl.BlockSpec(memory_space=pltpu.VMEM)],
        out_specs=pl.BlockSpec(memory_space=pltpu.VMEM),
        scratch_shapes=[
            pltpu.VMEM((holders, rows, LANES), jnp.float32),
            pltpu.SemaphoreType.DMA((holders,)),
            pltpu.SemaphoreType.DMA((holders,)),
        ],
        compiler_params=pltpu.CompilerParams(
            collective_id=0, has_side_effects=True, vmem_limit_bytes=32 * 1024 * 1024
        ),
    )(gradient)


def matmul(left, right):
    return jnp.dot(left, right, preferred_element_type=jnp.float32)


def halves(wide):
    high = wide.astype(jnp.bfloat16)
    return high, (wide - high.astype(jnp.float32)).astype(jnp.bfloat16)


def eye_of(order):
    return jnp.where(
        lax.broadcasted_iota(jnp.int32, (order, order), 0)
        == lax.broadcasted_iota(jnp.int32, (order, order), 1),
        1.0,
        0.0,
    ).astype(jnp.float32)


def total_of(wide):
    return jnp.sum(jnp.sum(wide, axis=0, keepdims=True), axis=1, keepdims=True)


def root_kernel(holders, ids_ref, grad_ref, map_ref, trace_ref, root_ref):
    together, order, columns = grad_ref.shape
    first = pl.program_id(0) * together
    holder = lax.axis_index("mp")
    eye = eye_of(order)
    layers = map_ref[...]
    traces = trace_ref[0 : layers.shape[0], :]
    state = []
    for j in range(together):
        block = (first + j) * holders + holder
        layer = ids_ref[block]
        same = layers == layer
        total = total_of(jnp.where(same, traces, 0.0))
        count = total_of(jnp.where(same, 1.0, 0.0))
        ridge = 0.1 * total / (count * order)
        grad = grad_ref[j]
        stats = lax.dot_general(
            grad, grad, (((1,), (1,)), ((), ())), preferred_element_type=jnp.float32
        ) * (1.0 / columns)
        damped = stats + ridge * eye
        scaled = 2.5 / jnp.sqrt(total_of(damped * damped))
        m = scaled * (total_of(damped * eye) * (1.0 / order))
        h = scaled * damped - m * eye
        state.append((m, h, jnp.sqrt(jnp.sqrt(scaled)), None))
    for k in range(ITERS):
        after = []
        for m, h, x, y in state:
            if k in RECENTRE:
                shift = total_of(h * eye) * (1.0 / order)
                m = m + shift
                h = h - shift * eye
            f = 1.25 - 0.25 * m
            high, low = halves(h)
            if k == 0:
                y = (-0.25 * x) * h
            else:
                y = f * y + (-0.25 * x) * h - 0.25 * matmul(y.astype(jnp.bfloat16), high)
            x = x * f
            if k < ITERS - 1:
                e = (-0.5 * f) * h + 0.0625 * matmul(high, high)
                eb = e.astype(jnp.bfloat16)
                s = f * f
                g = (2.0 * s) * e + matmul(eb, eb)
                t = s * s
                ghigh, glow = halves(g)
                h = (
                    t * h
                    + m * g
                    + (matmul(ghigh, high) + matmul(ghigh, low) + matmul(glow, high))
                )
                m = t * m
            after.append((m, h, x, y))
        state = after
    for j in range(together):
        m, h, x, y = state[j]
        root_ref[j] = y + x * eye


def local_whole(grads, layer_map):
    gradient = grads[0, :, 0]
    blocks_here, order, columns = gradient.shape
    holders = lax.axis_size("mp")
    blocks = blocks_here * holders
    traces = exchange_traces(gradient, holders, blocks)
    together = TOGETHER if blocks_here % TOGETHER == 0 else 1
    padded = -(-blocks // LANES) * LANES
    layers = jnp.pad(layer_map, (0, padded - blocks), constant_values=-1).reshape(-1, LANES)
    roots = pl.pallas_call(
        functools.partial(root_kernel, holders),
        out_shape=jax.ShapeDtypeStruct((blocks_here, order, order), jnp.float32),
        grid_spec=pltpu.PrefetchScalarGridSpec(
            num_scalar_prefetch=1,
            grid=(blocks_here // together,),
            in_specs=[
                pl.BlockSpec((together, order, columns), lambda i, ids: (i, 0, 0)),
                pl.BlockSpec(layers.shape, lambda i, ids: (0, 0)),
                pl.BlockSpec(traces.shape, lambda i, ids: (0, 0)),
            ],
            out_specs=pl.BlockSpec((together, order, order), lambda i, ids: (i, 0, 0)),
        ),
        compiler_params=pltpu.CompilerParams(vmem_limit_bytes=48 * 1024 * 1024),
    )(layer_map, gradient, layers, traces)
    return roots.reshape(blocks_here, 1, order, order)


def local(grads, layer_map):
    if lax.axis_size("dp") == 1:
        return local_whole(grads, layer_map)
    return local_split(grads, layer_map)


def solution(mesh):
    placed = (P("dp", None, "mp", None, None), P())
    return jax.shard_map(
        local, mesh=mesh, in_specs=placed, out_specs=P(None, "mp", "dp", None), check_vma=False
    )
```

```python
import functools

import jax
import jax.numpy as jnp
from jax import lax
from jax.experimental import pallas as pl
from jax.experimental.pallas import tpu as pltpu
from jax.sharding import PartitionSpec as P

ITERS = 8


def newton_root(stats, ridge, live):
    order = stats.shape[-1]
    identity = jnp.eye(order, dtype=jnp.float32)
    damped = jnp.where(live[:, None, None], stats + ridge[:, None, None] * identity, identity)
    frobenius = jnp.sqrt(jnp.sum(damped * damped, axis=(1, 2)))
    scaled = 2.5 / frobenius
    current = (scaled**0.25)[:, None, None] * identity
    coupled = scaled[:, None, None] * damped
    for _ in range(ITERS):
        factor = 1.25 * identity - 0.25 * coupled
        current = jnp.einsum("sij,sjk->sik", current, factor, precision=lax.Precision.HIGHEST)
        square = jnp.einsum("sij,sjk->sik", factor, factor, precision=lax.Precision.HIGHEST)
        fourth = jnp.einsum("sij,sjk->sik", square, square, precision=lax.Precision.HIGHEST)
        coupled = jnp.einsum("sij,sjk->sik", fourth, coupled, precision=lax.Precision.HIGHEST)
    return current


def local_split(grads, layer_map):
    gradient = grads[0, :, 0]
    blocks_here, order, columns = gradient.shape
    replicas = lax.axis_size("dp")
    holders = lax.axis_size("mp")
    band = order // replicas
    replica = lax.axis_index("dp")
    holder = lax.axis_index("mp")
    partial_value = jnp.einsum(
        "bic,bjc->bij", gradient, gradient, preferred_element_type=jnp.float32
    ) * (1.0 / (replicas * columns))
    summed = lax.psum(partial_value, "dp")
    mine = lax.dynamic_slice_in_dim(summed, replica * band, band, 1)
    layer_grid = layer_map.reshape(blocks_here, holders)
    my_layers = lax.dynamic_slice_in_dim(layer_grid, holder, 1, 1)[:, 0]
    layer_ids = jnp.arange(holders, dtype=jnp.int32)
    local_onehot = (my_layers[:, None] == layer_ids[None, :]).astype(jnp.float32)
    all_counts = jnp.sum((layer_map[:, None] == layer_ids[None, :]).astype(jnp.int32), axis=0)
    diag_rows = lax.dynamic_slice_in_dim(mine, replica * band, band, 2)
    diag_part = jnp.trace(diag_rows, axis1=1, axis2=2)
    layer_part = jnp.dot(diag_part, local_onehot, precision=lax.Precision.HIGHEST)
    layer_total = lax.psum(layer_part, ("dp", "mp"))
    layer_ridge = 0.1 * layer_total / (all_counts.astype(jnp.float32) * order)
    spread = -(-blocks_here // replicas)
    extra = replicas * spread - blocks_here
    stacked = lax.all_to_all(mine, "dp", split_axis=0, concat_axis=1, tiled=True)
    block_ridge = jnp.pad(
        jnp.dot(local_onehot, layer_ridge, precision=lax.Precision.HIGHEST), (0, extra)
    )
    slot_ridge = lax.dynamic_slice_in_dim(block_ridge, replica * spread, spread, 0)
    slot_index = replica * spread + jnp.arange(spread, dtype=jnp.int32)
    solved = newton_root(stacked, slot_ridge, slot_index < blocks_here)
    returned = lax.all_to_all(solved, "dp", split_axis=1, concat_axis=0, tiled=True)
    result = returned[:blocks_here]
    return result.reshape(blocks_here, 1, band, order)


LANES = 128
TOGETHER = 4
RECENTRE = (2, 4, 6)


def trace_exchange(holders, grad_ref, total_ref, slots, send_sem, recv_sem):
    me = lax.axis_index("mp")
    peers = [lax.rem(me + step, holders) for step in range(1, holders)]
    barrier = pltpu.get_barrier_semaphore()
    for peer in peers:
        pl.semaphore_signal(
            barrier, inc=1, device_id={"mp": peer}, device_id_type=pl.DeviceIdType.MESH
        )
    blocks_here, _, columns = grad_ref.shape
    shape = total_ref.shape
    place = lax.broadcasted_iota(jnp.int32, shape, 0) * LANES + lax.broadcasted_iota(
        jnp.int32, shape, 1
    )
    mine = jnp.zeros(shape, jnp.float32)
    for i in range(blocks_here):
        wide = grad_ref[i].astype(jnp.float32)
        rows = jnp.sum(wide * wide, axis=0, keepdims=True)
        trace = jnp.sum(rows, axis=1, keepdims=True) * (1.0 / columns)
        mine = jnp.where(place == i * holders + me, trace, mine)
    slots[me] = mine
    pl.semaphore_wait(barrier, holders - 1)
    copies = []
    for peer in peers:
        copy = pltpu.make_async_remote_copy(
            src_ref=slots.at[me],
            dst_ref=slots.at[me],
            send_sem=send_sem.at[peer],
            recv_sem=recv_sem.at[me],
            device_id={"mp": peer},
            device_id_type=pl.DeviceIdType.MESH,
        )
        copy.start()
        copies.append(copy)
    for peer in peers:
        pltpu.make_async_remote_copy(
            src_ref=slots.at[peer],
            dst_ref=slots.at[peer],
            send_sem=send_sem.at[peer],
            recv_sem=recv_sem.at[peer],
            device_id={"mp": peer},
            device_id_type=pl.DeviceIdType.MESH,
        ).wait_recv()
    total = slots[0]
    for i in range(1, holders):
        total = total + slots[i]
    total_ref[...] = total
    for copy in copies:
        copy.wait_send()


def exchange_traces(gradient, holders, blocks):
    rows = -(-blocks // (8 * LANES)) * 8
    return pl.pallas_call(
        functools.partial(trace_exchange, holders),
        out_shape=jax.ShapeDtypeStruct((rows, LANES), jnp.float32),
        in_specs=[pl.BlockSpec(memory_space=pltpu.VMEM)],
        out_specs=pl.BlockSpec(memory_space=pltpu.VMEM),
        scratch_shapes=[
            pltpu.VMEM((holders, rows, LANES), jnp.float32),
            pltpu.SemaphoreType.DMA((holders,)),
            pltpu.SemaphoreType.DMA((holders,)),
        ],
        compiler_params=pltpu.CompilerParams(
            collective_id=0, has_side_effects=True, vmem_limit_bytes=32 * 1024 * 1024
        ),
    )(gradient)


def matmul(left, right):
    return jnp.dot(left, right, preferred_element_type=jnp.float32)


def halves(wide):
    high = wide.astype(jnp.bfloat16)
    return high, (wide - high.astype(jnp.float32)).astype(jnp.bfloat16)


def eye_of(order):
    return jnp.where(
        lax.broadcasted_iota(jnp.int32, (order, order), 0)
        == lax.broadcasted_iota(jnp.int32, (order, order), 1),
        1.0,
        0.0,
    ).astype(jnp.float32)


def total_of(wide):
    return jnp.sum(jnp.sum(wide, axis=0, keepdims=True), axis=1, keepdims=True)


def root_kernel(holders, ids_ref, grad_ref, map_ref, trace_ref, root_ref):
    together, order, columns = grad_ref.shape
    first = pl.program_id(0) * together
    holder = lax.axis_index("mp")
    eye = eye_of(order)
    layers = map_ref[...]
    traces = trace_ref[0 : layers.shape[0], :]
    m, h, x, y = [], [], [], []
    for j in range(together):
        block = (first + j) * holders + holder
        layer = ids_ref[block]
        same = layers == layer
        total = total_of(jnp.where(same, traces, 0.0))
        count = total_of(jnp.where(same, 1.0, 0.0))
        ridge = 0.1 * total / (count * order)
        grad = grad_ref[j]
        stats = lax.dot_general(
            grad, grad, (((1,), (1,)), ((), ())), preferred_element_type=jnp.float32
        ) * (1.0 / columns)
        damped = stats + ridge * eye
        scaled = 2.5 / jnp.sqrt(total_of(damped * damped))
        m.append(scaled * (total_of(damped * eye) * (1.0 / order)))
        h.append(scaled * damped - m[j] * eye)
        x.append(jnp.sqrt(jnp.sqrt(scaled)))
        y.append(None)
    every = range(together)
    for k in range(ITERS):
        last = k == ITERS - 1
        if k in RECENTRE:
            for j in every:
                shift = total_of(h[j] * eye) * (1.0 / order)
                m[j] = m[j] + shift
                h[j] = h[j] - shift * eye
        f = [1.25 - 0.25 * m[j] for j in every]
        high, low, eb, e, g, ghigh, glow = ([None] * together for _ in range(7))
        for j in every:
            high[j], low[j] = halves(h[j])
            if not last:
                e[j] = (-0.5 * f[j]) * h[j] + 0.0625 * matmul(high[j], high[j])
                eb[j] = e[j].astype(jnp.bfloat16)
        for j in every:
            if k == 0:
                y[j] = (-0.25 * x[j]) * h[j]
            else:
                yb = y[j].astype(jnp.bfloat16)
                y[j] = f[j] * y[j] + (-0.25 * x[j]) * h[j] - 0.25 * matmul(yb, high[j])
            x[j] = x[j] * f[j]
            if not last:
                s = f[j] * f[j]
                g[j] = (2.0 * s) * e[j] + matmul(eb[j], eb[j])
                ghigh[j], glow[j] = halves(g[j])
        if last:
            break
        for j in every:
            t = f[j] * f[j] * f[j] * f[j]
            product = matmul(
                jnp.concatenate([ghigh[j], ghigh[j], glow[j]], axis=1),
                jnp.concatenate([high[j], low[j], high[j]], axis=0),
            )
            h[j] = t * h[j] + m[j] * g[j] + product
            m[j] = t * m[j]
    for j in every:
        root_ref[j] = y[j] + x[j] * eye


def local_whole(grads, layer_map):
    gradient = grads[0, :, 0]
    blocks_here, order, columns = gradient.shape
    holders = lax.axis_size("mp")
    blocks = blocks_here * holders
    traces = exchange_traces(gradient, holders, blocks)
    together = TOGETHER if blocks_here % TOGETHER == 0 else 1
    padded = -(-blocks // LANES) * LANES
    layers = jnp.pad(layer_map, (0, padded - blocks), constant_values=-1).reshape(-1, LANES)
    roots = pl.pallas_call(
        functools.partial(root_kernel, holders),
        out_shape=jax.ShapeDtypeStruct((blocks_here, order, order), jnp.float32),
        grid_spec=pltpu.PrefetchScalarGridSpec(
            num_scalar_prefetch=1,
            grid=(blocks_here // together,),
            in_specs=[
                pl.BlockSpec((together, order, columns), lambda i, ids: (i, 0, 0)),
                pl.BlockSpec(layers.shape, lambda i, ids: (0, 0)),
                pl.BlockSpec(traces.shape, lambda i, ids: (0, 0)),
            ],
            out_specs=pl.BlockSpec((together, order, order), lambda i, ids: (i, 0, 0)),
        ),
        compiler_params=pltpu.CompilerParams(vmem_limit_bytes=60 * 1024 * 1024),
    )(layer_map, gradient, layers, traces)
    return roots.reshape(blocks_here, 1, order, order)


def local(grads, layer_map):
    if lax.axis_size("dp") == 1:
        return local_whole(grads, layer_map)
    return local_split(grads, layer_map)


def solution(mesh):
    placed = (P("dp", None, "mp", None, None), P())
    return jax.shard_map(
        local, mesh=mesh, in_specs=placed, out_specs=P(None, "mp", "dp", None), check_vma=False
    )
```
